256 devices in a mesh: grid: 128 (over z, y_hi, x, core), vec: 2 (over y_lo).
Axes of the slice: x: 4, y: 4 (y_hi: 2, y_lo: 2; y = y_hi * 2 + y_lo), z: 8, core: 2. Of those that a mesh axis runs over, the one named last changes fastest.
Arguments:
- vectors: bfloat16 [16, 32768], P('vec', 'grid'), may hold values from -6 to 6
- tile_blocks: bfloat16 [6144, 256, 256], P('grid'), may hold values from -0.0546875 to 0.0546875
- tile_rows: int32 [6144], P('grid'), may hold values from 0 to 127, as said below
- tile_cols: int32 [6144], P('grid'), may hold values from 0 to 127, as said below
- tile_counts: int32 [128], P('grid'), may hold values from 6 to 48, as said below
Outputs:
- product: float32 [16, 32768], P('vec', 'grid')
The draws below stay inside these ranges and needn't reach their ends.
Inputs may be any that keep to these rules, and one draw needn't show every extreme that they name: `tile_rows`: owner g = s // 48 of slot s has row range a = g // 8; its tiles lie in block rows a * 8 to (a + 1) * 8 - 1. `tile_cols`: owner g has column range c = (g // 8 + (g % 8) * 2) mod 16; its tiles lie in block columns c * 8 to (c + 1) * 8 - 1. `tile_counts`: the live tiles of an owner are its first slots; at least one owner is full.
All inputs are finite; a program needn't handle non-finite values.
Results may differ from the reference program's by a relative error of at most 0.0003.
Values may be sent and summed in bfloat16 or wider, within the bound.
A program may use at most 64 MiB of HBM per device.

```python
import jax
import jax.numpy as jnp
from jax import lax

B = 256
NVEC = 16
BLK_DEV = 1
SLOTS = 48
GROUP = 8
NRANGE = 16
NROWS = 32768
NTILES = 6144
N_GRID = 128


def coordinate_pair(key):
    slot_ids = jnp.arange(NTILES, dtype=jnp.int32)
    owner = slot_ids // SLOTS
    row_range = owner // GROUP
    col_range = (row_range + owner % GROUP * (NRANGE // GROUP)) % NRANGE
    span = GROUP * BLK_DEV
    row_ids = row_range * span + jax.random.randint(jax.random.fold_in(key, 11), (NTILES,), 0, span)
    col_ids = col_range * span + jax.random.randint(jax.random.fold_in(key, 12), (NTILES,), 0, span)
    return (row_ids, col_ids)


def draw_tile_rows(key, part):
    row_ids, col_ids = coordinate_pair(key)
    return row_ids.astype(jnp.int32)


def draw_tile_cols(key, part):
    row_ids, col_ids = coordinate_pair(key)
    return col_ids.astype(jnp.int32)


def draw_tile_counts(key, part):
    key = jax.random.fold_in(key, 5)
    levels = jax.random.randint(jax.random.fold_in(key, 1), (N_GRID,), 0, 4)
    divisor = jnp.array([1, 2, 4, 8], dtype=jnp.int32)[levels]
    counts = SLOTS // divisor
    fullest = jax.random.randint(jax.random.fold_in(key, 2), (), 0, N_GRID)
    return counts.at[fullest].set(SLOTS).astype(jnp.int32)


def block_levels(key, extent, pieces, smallest, top_value):
    factor_of = 1.0
    for dim, parts in pieces:
        heights = jax.random.uniform(jax.random.fold_in(jax.random.fold_in(key, 6), dim), (parts,), jnp.float32, smallest / len(pieces), top_value / len(pieces))
        factor_of = factor_of * jnp.repeat(jnp.exp(heights), extent[dim] // parts).reshape((-1,) + (1,) * (len(extent) - 1 - dim))
    return factor_of


def noise(rng, extent, width, limit, pieces=(), kind=jnp.bfloat16):
    loudness = block_levels(rng, extent, pieces, -0.22, 0.18) if pieces else 1.0
    drawn = jax.random.normal(rng, extent, jnp.float32) * width * loudness
    return jnp.minimum(jnp.maximum(drawn, -limit), limit).astype(kind)


def setup_inputs(seed: int = 0) -> dict:
    key_of = jax.random.split(jax.random.key(seed), 6)
    return {
        "vectors": noise(key_of[0], (NVEC, NROWS), 1.0, 6.0, ((0, 2), (1, 128))),
        "tile_blocks": noise(key_of[1], (NTILES, B, B), (B * SLOTS) ** -0.5, 0.0546875, ((0, 128),)),
        "tile_rows": draw_tile_rows(jax.random.fold_in(key_of[5], 71), 0),
        "tile_cols": draw_tile_cols(jax.random.fold_in(key_of[5], 71), 0),
        "tile_counts": draw_tile_counts(jax.random.fold_in(key_of[5], 71), 0),
    }


def reference(vectors, tile_blocks, tile_rows, tile_cols, tile_counts):
    nrows = vectors.shape[1]
    nblocks = nrows // B
    vec_blocks = vectors.astype(jnp.float32).reshape(NVEC, nblocks, B).transpose(1, 0, 2)
    ntiles = tile_blocks.shape[0]
    owner = jnp.arange(ntiles, dtype=jnp.int32) // SLOTS
    within = jnp.arange(ntiles, dtype=jnp.int32) % SLOTS
    live_mask = (within < tile_counts[owner]).astype(jnp.float32)
    group_size = 16

    def visit(counter, running):
        offset = (counter * group_size).astype(jnp.int32)
        tile_set = lax.dynamic_slice_in_dim(tile_blocks, offset, group_size, 0).astype(jnp.float32)
        row_ids = lax.dynamic_slice_in_dim(tile_rows, offset, group_size, 0)
        col_ids = lax.dynamic_slice_in_dim(tile_cols, offset, group_size, 0)
        keep_mask = lax.dynamic_slice_in_dim(live_mask, offset, group_size, 0)[:, None, None]
        col_vecs = vec_blocks[col_ids]
        row_vecs = vec_blocks[row_ids]
        direct = jnp.einsum("gij,gvj->gvi", tile_set, col_vecs) * keep_mask
        mirror = jnp.einsum("gij,gvi->gvj", tile_set, row_vecs) * keep_mask
        running = running.at[row_ids].add(direct)
        return running.at[col_ids].add(mirror)

    running = jnp.zeros((nblocks, NVEC, B), jnp.float32)
    running = lax.fori_loop(0, ntiles // group_size, visit, running)
    return running.transpose(1, 0, 2).reshape(NVEC, nrows)
```

```python
import jax
import jax.numpy as jnp
from jax import lax
from jax.experimental import pallas as pl
from jax.experimental.pallas import tpu as pltpu
from jax.sharding import PartitionSpec as P

B = 256
GROUP = 8
NRANGE = 16
STEP = NRANGE // GROUP
SLOTS = 48
CHUNK = 8
NCHUNK = SLOTS // CHUNK
ROWS = GROUP * 8
DEAD = GROUP * GROUP
MESH = pl.DeviceIdType.MESH


def kernel(
    x_ref,
    tiles_ref,
    rows_ref,
    cols_ref,
    count_ref,
    out_ref,
    tiles,
    slabs,
    placed,
    acc,
    sums,
    tile_sem,
    send_sem,
    recv_sem,
):
    me = lax.axis_index("grid")
    a = me // GROUP
    j = me % GROUP
    c = (a + STEP * j) % NRANGE
    far = j != 0

    def tile_copy(n):
        part = pl.ds(n * CHUNK, CHUNK)
        return pltpu.make_async_copy(tiles_ref.at[part], tiles.at[part], tile_sem.at[n])

    for n in range(NCHUNK):
        tile_copy(n).start()

    row_peers = [a * GROUP + (j + d) % GROUP for d in range(1, GROUP)]
    owners = [
        ((a + NRANGE - STEP * d) % NRANGE) * GROUP + d for d in range(1, GROUP)
    ]
    col_peers = [c * GROUP + k for k in range(GROUP)]

    barrier = pltpu.get_barrier_semaphore()
    for peer in row_peers + owners:
        pl.semaphore_signal(barrier, inc=1, device_id={"grid": peer}, device_id_type=MESH)

    @pl.when(far)
    def _():
        for peer in col_peers:
            pl.semaphore_signal(
                barrier, inc=1, device_id={"grid": peer}, device_id_type=MESH
            )

    own = x_ref[...]
    slabs[j] = jnp.concatenate([own[:, :128], own[:, 128:]], axis=0)
    placed[...] = jnp.zeros_like(placed)
    acc[...] = jnp.zeros_like(acc)

    pl.semaphore_wait(barrier, 2 * (GROUP - 1) + jnp.where(far, GROUP, 0))

    def x_copy(n, peer, slot):
        return pltpu.make_async_remote_copy(
            src_ref=slabs.at[j],
            dst_ref=slabs.at[slot],
            send_sem=send_sem.at[n],
            recv_sem=recv_sem.at[slot],
            device_id={"grid": peer},
            device_id_type=MESH,
        )

    x_sends = [x_copy(n, peer, j) for n, peer in enumerate(row_peers)]
    x_sends += [x_copy(GROUP - 1 + n, peer, GROUP + j) for n, peer in enumerate(owners)]
    for copy in x_sends:
        copy.start()

    def arrived(slot):
        pltpu.make_async_remote_copy(
            src_ref=slabs.at[slot],
            dst_ref=slabs.at[slot],
            send_sem=send_sem.at[0],
            recv_sem=recv_sem.at[slot],
            device_id={"grid": row_peers[0]},
            device_id_type=MESH,
        ).wait_recv()

    def place(side, first):
        for k in range(GROUP):
            slab = slabs[first + k].astype(jnp.float32)
            block = jnp.concatenate([slab[:8], slab[8:]], axis=1)
            blank = jnp.zeros_like(block)
            low = jnp.concatenate([block, blank], axis=0).astype(jnp.bfloat16)
            high = jnp.concatenate([blank, block], axis=0).astype(jnp.bfloat16)
            for t in range(GROUP):
                rows = pl.ds(t // 2 * 16, 16)
                placed[side, GROUP * k + t, rows, :] = high if t % 2 else low

    live_count = count_ref[0]

    def coords(slot):
        return rows_ref[slot] - a * GROUP, cols_ref[slot] - c * GROUP

    def spread(side, slot, source, target):
        return placed[side, jnp.where(slot < live_count, GROUP * source + target, DEAD)]

    for d in range(1, GROUP):
        arrived((j + d) % GROUP)
    place(0, 0)

    def mirror(n, carry):
        tile_copy(n).wait()
        total = acc[1]
        for t in range(CHUNK):
            slot = n * CHUNK + t
            r, q = coords(slot)
            total += jnp.dot(
                spread(0, slot, r, q), tiles[slot], preferred_element_type=jnp.float32
            )
        acc[1] = total
        return carry

    lax.fori_loop(0, NCHUNK, mirror, 0)

    def sum_copy(n, side, block, peer, slot):
        return pltpu.make_async_remote_copy(
            src_ref=acc.at[side, pl.ds(pl.multiple_of(block * 8, 8), 8)],
            dst_ref=sums.at[slot],
            send_sem=send_sem.at[n],
            recv_sem=recv_sem.at[2 * GROUP + slot],
            device_id={"grid": peer},
            device_id_type=MESH,
        )

    col_sends = [
        sum_copy(2 * (GROUP - 1) + k, 1, k, peer, GROUP + j)
        for k, peer in enumerate(col_peers)
    ]

    @pl.when(far)
    def _():
        for copy in col_sends:
            copy.start()
        for k in range(GROUP):
            arrived(GROUP + k)

    place(1, jnp.where(far, GROUP, 0))

    @pl.when(j == 0)
    def _():
        acc[0] = acc[1]

    def direct(n, carry):
        total = acc[0]
        for t in range(CHUNK):
            slot = n * CHUNK + t
            r, q = coords(slot)
            total += lax.dot_general(
                spread(1, slot, q, r),
                tiles[slot],
                (((1,), (1,)), ((), ())),
                preferred_element_type=jnp.float32,
            )
        acc[0] = total
        return carry

    lax.fori_loop(0, NCHUNK, direct, 0)

    row_sends = [
        sum_copy(2 * (GROUP - 1) + GROUP + n, 0, (j + n + 1) % GROUP, peer, j)
        for n, peer in enumerate(row_peers)
    ]
    for copy in row_sends:
        copy.start()

    def sum_arrived(slot):
        pltpu.make_async_remote_copy(
            src_ref=sums.at[slot],
            dst_ref=sums.at[slot],
            send_sem=send_sem.at[0],
            recv_sem=recv_sem.at[2 * GROUP + slot],
            device_id={"grid": row_peers[0]},
            device_id_type=MESH,
        ).wait_recv()

    result = acc[0, pl.ds(pl.multiple_of(j * 8, 8), 8), :]
    for d in range(1, GROUP):
        sum_arrived(GROUP + d)
        result += sums[GROUP + d]
    for d in range(1, GROUP):
        slot = (j + d) % GROUP
        sum_arrived(slot)
        result += sums[slot]
    out_ref[...] = result

    for copy in x_sends + row_sends:
        copy.wait_send()

    @pl.when(far)
    def _():
        for copy in col_sends:
            copy.wait_send()


def per_device(vectors, tile_blocks, tile_rows, tile_cols, tile_counts):
    smem = pl.BlockSpec(memory_space=pltpu.SMEM)
    vmem = pl.BlockSpec(memory_space=pltpu.VMEM)
    return pl.pallas_call(
        kernel,
        out_shape=jax.ShapeDtypeStruct((8, B), jnp.float32),
        in_specs=[vmem, pl.BlockSpec(memory_space=pl.ANY), smem, smem, smem],
        out_specs=vmem,
        scratch_shapes=[
            pltpu.VMEM((SLOTS, B, B), jnp.bfloat16),
            pltpu.VMEM((2 * GROUP, 16, 128), jnp.bfloat16),
            pltpu.VMEM((2, DEAD + 1, ROWS, B), jnp.bfloat16),
            pltpu.VMEM((2, ROWS, B), jnp.float32),
            pltpu.VMEM((2 * GROUP, 8, B), jnp.float32),
            pltpu.SemaphoreType.DMA((NCHUNK,)),
            pltpu.SemaphoreType.DMA((3 * GROUP + 2 * GROUP,)),
            pltpu.SemaphoreType.DMA((4 * GROUP,)),
        ],
        compiler_params=pltpu.CompilerParams(
            collective_id=0, has_side_effects=True, vmem_limit_bytes=60 * 1024 * 1024
        ),
        cost_estimate=pl.CostEstimate(
            flops=4 * SLOTS * B * B * 8, bytes_accessed=SLOTS * B * B * 2, transcendentals=0
        ),
    )(vectors, tile_blocks, tile_rows, tile_cols, tile_counts)


def solution(mesh):
    return jax.shard_map(
        per_device,
        mesh=mesh,
        in_specs=(P("vec", "grid"), P("grid", None, None), P("grid"), P("grid"), P("grid")),
        out_specs=P("vec", "grid"),
        check_vma=False,
    )
```

```python
import jax
import jax.numpy as jnp
from jax import lax
from jax.experimental import pallas as pl
from jax.experimental.pallas import tpu as pltpu
from jax.sharding import PartitionSpec as P

B = 256
GROUP = 8
NRANGE = 16
STEP = NRANGE // GROUP
SLOTS = 48
CHUNK = 8
NCHUNK = SLOTS // CHUNK
ROWS = GROUP * 8
DEAD = GROUP * GROUP
MESH = pl.DeviceIdType.MESH


def kernel(
    x_hbm,
    tiles_ref,
    rows_hbm,
    cols_hbm,
    count_ref,
    out_ref,
    x_ref,
    rows_ref,
    cols_ref,
    tiles,
    slabs,
    placed,
    acc,
    sums,
    in_sem,
    tile_sem,
    send_sem,
    recv_sem,
):
    me = lax.axis_index("grid")
    a = me // GROUP
    j = me % GROUP
    c = (a + STEP * j) % NRANGE
    far = j != 0

    def tile_copy(n):
        part = pl.ds(n * CHUNK, CHUNK)
        return pltpu.make_async_copy(tiles_ref.at[part], tiles.at[part], tile_sem.at[n])

    row_peers = [a * GROUP + (j + d) % GROUP for d in range(1, GROUP)]
    owners = [
        ((a + NRANGE - STEP * d) % NRANGE) * GROUP + d for d in range(1, GROUP)
    ]
    col_peers = [c * GROUP + k for k in range(GROUP)]

    barrier = pltpu.get_barrier_semaphore()

    @pl.when(far)
    def _():
        for peer in col_peers:
            pl.semaphore_signal(
                barrier, inc=1, device_id={"grid": peer}, device_id_type=MESH
            )

    for peer in row_peers:
        pl.semaphore_signal(barrier, inc=1, device_id={"grid": peer}, device_id_type=MESH)

    inputs = [
        pltpu.make_async_copy(source, target, in_sem.at[n])
        for n, (source, target) in enumerate(
            [(x_hbm, x_ref), (rows_hbm, rows_ref), (cols_hbm, cols_ref)]
        )
    ]
    for copy in inputs:
        copy.start()
    for n in range(NCHUNK):
        tile_copy(n).start()

    placed[...] = jnp.zeros_like(placed)
    acc[...] = jnp.zeros_like(acc)
    for copy in inputs:
        copy.wait()
    own = x_ref[...]
    slabs[j] = jnp.concatenate([own[:, :128], own[:, 128:]], axis=0)
    pl.semaphore_wait(barrier, 2 * (GROUP - 1))

    def x_copy(n, peer, slot):
        return pltpu.make_async_remote_copy(
            src_ref=slabs.at[j],
            dst_ref=slabs.at[slot],
            send_sem=send_sem.at[n],
            recv_sem=recv_sem.at[slot],
            device_id={"grid": peer},
            device_id_type=MESH,
        )

    x_sends = [x_copy(n, peer, j) for n, peer in enumerate(row_peers)]
    x_sends += [x_copy(GROUP - 1 + n, peer, GROUP + j) for n, peer in enumerate(owners)]
    for copy in x_sends:
        copy.start()

    def arrived(slot):
        pltpu.make_async_remote_copy(
            src_ref=slabs.at[slot],
            dst_ref=slabs.at[slot],
            send_sem=send_sem.at[0],
            recv_sem=recv_sem.at[slot],
            device_id={"grid": row_peers[0]},
            device_id_type=MESH,
        ).wait_recv()

    def place(side, first):
        for k in range(GROUP):
            slab = slabs[first + k].astype(jnp.float32)
            block = jnp.concatenate([slab[:8], slab[8:]], axis=1)
            blank = jnp.zeros_like(block)
            low = jnp.concatenate([block, blank], axis=0).astype(jnp.bfloat16)
            high = jnp.concatenate([blank, block], axis=0).astype(jnp.bfloat16)
            for t in range(GROUP):
                rows = pl.ds(t // 2 * 16, 16)
                placed[side, GROUP * k + t, rows, :] = high if t % 2 else low

    live_count = count_ref[0]

    def coords(slot):
        return rows_ref[slot] - a * GROUP, cols_ref[slot] - c * GROUP

    def spread(side, slot, source, target):
        return placed[side, jnp.where(slot < live_count, GROUP * source + target, DEAD)]

    for d in range(1, GROUP):
        arrived((j + d) % GROUP)
    place(0, 0)

    def mirror(n, carry):
        tile_copy(n).wait()
        total = acc[1]
        for t in range(CHUNK):
            slot = n * CHUNK + t
            r, q = coords(slot)
            total += jnp.dot(
                spread(0, slot, r, q), tiles[slot], preferred_element_type=jnp.float32
            )
        acc[1] = total
        return carry

    lax.fori_loop(0, NCHUNK, mirror, 0)

    def sum_copy(n, side, block, peer, slot):
        return pltpu.make_async_remote_copy(
            src_ref=acc.at[side, pl.ds(pl.multiple_of(block * 8, 8), 8)],
            dst_ref=sums.at[slot],
            send_sem=send_sem.at[n],
            recv_sem=recv_sem.at[2 * GROUP + slot],
            device_id={"grid": peer},
            device_id_type=MESH,
        )

    col_sends = [
        sum_copy(2 * (GROUP - 1) + k, 1, k, peer, GROUP + j)
        for k, peer in enumerate(col_peers)
    ]

    @pl.when(far)
    def _():
        for k in range(GROUP):
            arrived(GROUP + k)
        for copy in col_sends:
            copy.start()

    place(1, jnp.where(far, GROUP, 0))

    @pl.when(j == 0)
    def _():
        acc[0] = acc[1]

    def direct(n, carry):
        total = acc[0]
        for t in range(CHUNK):
            slot = n * CHUNK + t
            r, q = coords(slot)
            total += lax.dot_general(
                spread(1, slot, q, r),
                tiles[slot],
                (((1,), (1,)), ((), ())),
                preferred_element_type=jnp.float32,
            )
        acc[0] = total
        return carry

    lax.fori_loop(0, NCHUNK, direct, 0)

    row_sends = [
        sum_copy(2 * (GROUP - 1) + GROUP + n, 0, (j + n + 1) % GROUP, peer, j)
        for n, peer in enumerate(row_peers)
    ]
    for copy in row_sends:
        copy.start()

    def sum_arrived(slot):
        pltpu.make_async_remote_copy(
            src_ref=sums.at[slot],
            dst_ref=sums.at[slot],
            send_sem=send_sem.at[0],
            recv_sem=recv_sem.at[2 * GROUP + slot],
            device_id={"grid": row_peers[0]},
            device_id_type=MESH,
        ).wait_recv()

    result = acc[0, pl.ds(pl.multiple_of(j * 8, 8), 8), :]
    for d in range(1, GROUP):
        sum_arrived(GROUP + d)
        result += sums[GROUP + d]
    for d in range(1, GROUP):
        slot = (j + d) % GROUP
        sum_arrived(slot)
        result += sums[slot]
    out_ref[...] = result

    for copy in x_sends + row_sends:
        copy.wait_send()

    @pl.when(far)
    def _():
        for copy in col_sends:
            copy.wait_send()


def per_device(vectors, tile_blocks, tile_rows, tile_cols, tile_counts):
    hbm = pl.BlockSpec(memory_space=pltpu.HBM)
    staged = [
        pltpu.with_memory_space_constraint(array, pltpu.HBM)
        for array in (vectors, tile_blocks, tile_rows, tile_cols)
    ]
    return pl.pallas_call(
        kernel,
        out_shape=pltpu.VMEM((8, B), jnp.float32),
        in_specs=[hbm] * 4 + [pl.BlockSpec(memory_space=pltpu.SMEM)],
        out_specs=pl.BlockSpec(memory_space=pltpu.VMEM),
        scratch_shapes=[
            pltpu.VMEM((8, B), jnp.bfloat16),
            pltpu.SMEM((SLOTS,), jnp.int32),
            pltpu.SMEM((SLOTS,), jnp.int32),
            pltpu.VMEM((SLOTS, B, B), jnp.bfloat16),
            pltpu.VMEM((2 * GROUP, 16, 128), jnp.bfloat16),
            pltpu.VMEM((2, DEAD + 1, ROWS, B), jnp.bfloat16),
            pltpu.VMEM((2, ROWS, B), jnp.float32),
            pltpu.VMEM((2 * GROUP, 8, B), jnp.float32),
            pltpu.SemaphoreType.DMA((3,)),
            pltpu.SemaphoreType.DMA((NCHUNK,)),
            pltpu.SemaphoreType.DMA((3 * GROUP + 2 * GROUP,)),
            pltpu.SemaphoreType.DMA((4 * GROUP,)),
        ],
        compiler_params=pltpu.CompilerParams(
            collective_id=0, has_side_effects=True, vmem_limit_bytes=32 * 1024 * 1024
        ),
        cost_estimate=pl.CostEstimate(
            flops=4 * SLOTS * B * B * 8, bytes_accessed=SLOTS * B * B * 2, transcendentals=0
        ),
    )(*staged, tile_counts)


def solution(mesh):
    return jax.shard_map(
        per_device,
        mesh=mesh,
        in_specs=(P("vec", "grid"), P("grid", None, None), P("grid"), P("grid"), P("grid")),
        out_specs=P("vec", "grid"),
        check_vma=False,
    )
```

```python
import jax
import jax.numpy as jnp
from jax import lax
from jax.experimental import pallas as pl
from jax.experimental.pallas import tpu as pltpu
from jax.sharding import PartitionSpec as P

B = 256
GROUP = 8
NRANGE = 16
STEP = NRANGE // GROUP
SLOTS = 48
CHUNK = 8
NCHUNK = SLOTS // CHUNK
ROWS = GROUP * 8
DEAD = GROUP * GROUP
MESH = pl.DeviceIdType.MESH


def kernel(
    x_hbm,
    tiles_ref,
    rows_hbm,
    cols_hbm,
    count_ref,
    out_ref,
    x_ref,
    rows_ref,
    cols_ref,
    tiles,
    slabs,
    placed,
    acc,
    sums,
    in_sem,
    tile_sem,
    send_sem,
    recv_sem,
):
    me = lax.axis_index("grid")
    a = me // GROUP
    j = me % GROUP
    c = (a + STEP * j) % NRANGE
    far = j != 0

    def tile_copy(n):
        part = pl.ds(n * CHUNK, CHUNK)
        return pltpu.make_async_copy(tiles_ref.at[part], tiles.at[part], tile_sem.at[n])

    row_peers = [a * GROUP + (j + d) % GROUP for d in range(1, GROUP)]
    owners = [
        ((a + NRANGE - STEP * d) % NRANGE) * GROUP + d for d in range(1, GROUP)
    ]
    col_peers = [c * GROUP + k for k in range(GROUP)]

    barrier = pltpu.get_barrier_semaphore()

    @pl.when(far)
    def _():
        for peer in col_peers:
            pl.semaphore_signal(
                barrier, inc=1, device_id={"grid": peer}, device_id_type=MESH
            )

    for peer in row_peers:
        pl.semaphore_signal(barrier, inc=1, device_id={"grid": peer}, device_id_type=MESH)

    inputs = [
        pltpu.make_async_copy(source, target, in_sem.at[n])
        for n, (source, target) in enumerate(
            [(x_hbm, x_ref), (rows_hbm, rows_ref), (cols_hbm, cols_ref)]
        )
    ]
    for copy in inputs:
        copy.start()
    for n in range(NCHUNK):
        tile_copy(n).start()

    placed[...] = jnp.zeros_like(placed)
    for copy in inputs:
        copy.wait()
    own = x_ref[...]
    slabs[j] = jnp.concatenate([own[:, :128], own[:, 128:]], axis=0)
    pl.semaphore_wait(barrier, 2 * (GROUP - 1))

    def send(source, target, n, peer):
        return pltpu.make_async_remote_copy(
            src_ref=source,
            dst_ref=target,
            send_sem=send_sem.at[n],
            recv_sem=recv_sem.at[n],
            device_id={"grid": peer},
            device_id_type=MESH,
        )

    def sum_block(side, k):
        return acc.at[side, pl.ds(pl.multiple_of(k * 8, 8), 8)]

    x_rows = [send(slabs.at[j], slabs.at[j], 0, peer) for peer in row_peers]
    x_cols = [send(slabs.at[j], slabs.at[GROUP + j], 1, peer) for peer in owners]
    sum_rows = [
        send(sum_block(0, (j + d) % GROUP), sums.at[j], 2, peer)
        for d, peer in enumerate(row_peers, 1)
    ]
    sum_cols = [
        send(sum_block(1, k), sums.at[GROUP + j], 3, peer)
        for k, peer in enumerate(col_peers)
    ]

    def several(buffer, count, n):
        part = buffer.at[pl.ds(0, count)]
        return send(part, part, n, row_peers[0])

    for copy in x_cols + x_rows:
        copy.start()

    def place(side, first):
        for k in range(GROUP):
            slab = slabs[first + k].astype(jnp.float32)
            block = jnp.concatenate([slab[:8], slab[8:]], axis=1)
            blank = jnp.zeros_like(block)
            low = jnp.concatenate([block, blank], axis=0).astype(jnp.bfloat16)
            high = jnp.concatenate([blank, block], axis=0).astype(jnp.bfloat16)
            for t in range(GROUP):
                rows = pl.ds(t // 2 * 16, 16)
                placed[side, GROUP * k + t, rows, :] = high if t % 2 else low

    live_count = count_ref[0]

    def coords(slot):
        return rows_ref[slot] - a * GROUP, cols_ref[slot] - c * GROUP

    def spread(side, slot, source, target):
        return placed[side, jnp.where(slot < live_count, GROUP * source + target, DEAD)]

    several(slabs, GROUP - 1, 0).wait_recv()
    place(0, 0)

    def mirror(n, total):
        for t in range(8):
            if t % CHUNK == 0:
                tile_copy(n * 1 + t // CHUNK).wait()
            slot = n * 8 + t
            r, q = coords(slot)
            total += jnp.dot(
                spread(0, slot, r, q), tiles[slot], preferred_element_type=jnp.float32
            )
        return total

    acc[1] = lax.fori_loop(0, 6, mirror, jnp.zeros((ROWS, B), jnp.float32))

    @pl.when(far)
    def _():
        several(slabs, GROUP, 1).wait_recv()
        for copy in sum_cols:
            copy.start()

    place(1, jnp.where(far, GROUP, 0))

    total = jnp.where(far, 0.0, acc[1])

    def direct(n, total):
        for t in range(8):
            slot = n * 8 + t
            r, q = coords(slot)
            total += lax.dot_general(
                spread(1, slot, q, r),
                tiles[slot],
                (((1,), (1,)), ((), ())),
                preferred_element_type=jnp.float32,
            )
        return total

    acc[0] = lax.fori_loop(0, 6, direct, total)

    for copy in sum_rows:
        copy.start()
    sums[j] = acc[0, pl.ds(pl.multiple_of(j * 8, 8), 8), :]
    several(sums, GROUP - 1, 3).wait_recv()
    result = sums[GROUP + 1]
    for k in range(GROUP + 2, 2 * GROUP):
        result += sums[k]
    several(sums, GROUP - 1, 2).wait_recv()
    for k in range(GROUP):
        result += sums[k]
    out_ref[...] = result

    several(slabs, GROUP - 1, 0).wait_send()
    several(slabs, GROUP - 1, 1).wait_send()
    several(sums, GROUP - 1, 2).wait_send()

    @pl.when(far)
    def _():
        several(sums, GROUP, 3).wait_send()


def per_device(vectors, tile_blocks, tile_rows, tile_cols, tile_counts):
    hbm = pl.BlockSpec(memory_space=pltpu.HBM)
    staged = [
        pltpu.with_memory_space_constraint(array, pltpu.HBM)
        for array in (vectors, tile_blocks, tile_rows, tile_cols)
    ]
    return pl.pallas_call(
        kernel,
        out_shape=pltpu.VMEM((8, B), jnp.float32),
        in_specs=[hbm] * 4 + [pl.BlockSpec(memory_space=pltpu.SMEM)],
        out_specs=pl.BlockSpec(memory_space=pltpu.VMEM),
        scratch_shapes=[
            pltpu.VMEM((8, B), jnp.bfloat16),
            pltpu.SMEM((SLOTS,), jnp.int32),
            pltpu.SMEM((SLOTS,), jnp.int32),
            pltpu.VMEM((SLOTS, B, B), jnp.bfloat16),
            pltpu.VMEM((2 * GROUP, 16, 128), jnp.bfloat16),
            pltpu.VMEM((2, DEAD + 1, ROWS, B), jnp.bfloat16),
            pltpu.VMEM((2, ROWS, B), jnp.float32),
            pltpu.VMEM((2 * GROUP, 8, B), jnp.float32),
            pltpu.SemaphoreType.DMA((3,)),
            pltpu.SemaphoreType.DMA((NCHUNK,)),
            pltpu.SemaphoreType.DMA((4,)),
            pltpu.SemaphoreType.DMA((4,)),
        ],
        compiler_params=pltpu.CompilerParams(
            collective_id=0, has_side_effects=True, vmem_limit_bytes=32 * 1024 * 1024
        ),
        cost_estimate=pl.CostEstimate(
            flops=4 * SLOTS * B * B * 8, bytes_accessed=SLOTS * B * B * 2, transcendentals=0
        ),
    )(*staged, tile_counts)


def solution(mesh):
    return jax.shard_map(
        per_device,
        mesh=mesh,
        in_specs=(P("vec", "grid"), P("grid", None, None), P("grid"), P("grid"), P("grid")),
        out_specs=P("vec", "grid"),
        check_vma=False,
    )
```

```python
import jax
import jax.numpy as jnp
from jax import lax
from jax.experimental import pallas as pl
from jax.experimental.pallas import tpu as pltpu
from jax.sharding import PartitionSpec as P

B = 256
GROUP = 8
NRANGE = 16
STEP = NRANGE // GROUP
SLOTS = 48
CHUNK = 8
NCHUNK = SLOTS // CHUNK
ROWS = GROUP * 8
DEAD = GROUP * GROUP
MESH = pl.DeviceIdType.MESH


def kernel(
    x_hbm,
    tiles_ref,
    rows_hbm,
    cols_hbm,
    count_ref,
    out_ref,
    x_ref,
    rows_ref,
    cols_ref,
    tiles,
    slabs,
    placed,
    acc,
    sums,
    in_sem,
    tile_sem,
    send_sem,
    recv_sem,
):
    me = lax.axis_index("grid")
    a = me // GROUP
    j = me % GROUP
    c = (a + STEP * j) % NRANGE
    far = j != 0

    def tile_copy(n):
        part = pl.ds(n * CHUNK, CHUNK)
        return pltpu.make_async_copy(tiles_ref.at[part], tiles.at[part], tile_sem.at[n])

    spots = [
        (j // 2 + x) % (GROUP // 2) * 2 + (j + core) % 2
        for x in (2, 1, 3, 0)
        for core in (0, 1)
    ]
    near = [k for n, k in enumerate(spots) if n != GROUP - 2]
    row_peers = [a * GROUP + k for k in near]
    owners = [
        ((a + NRANGE - STEP * d) % NRANGE) * GROUP + d for d in (4, 3, 5, 2, 6, 1, 7)
    ]
    col_peers = [c * GROUP + k for k in spots]

    barrier = pltpu.get_barrier_semaphore()

    @pl.when(far)
    def _():
        for peer in col_peers:
            pl.semaphore_signal(
                barrier, inc=1, device_id={"grid": peer}, device_id_type=MESH
            )

    for peer in owners + row_peers:
        pl.semaphore_signal(barrier, inc=1, device_id={"grid": peer}, device_id_type=MESH)

    inputs = [
        pltpu.make_async_copy(source, target, in_sem.at[n])
        for n, (source, target) in enumerate(
            [(x_hbm, x_ref), (rows_hbm, rows_ref), (cols_hbm, cols_ref)]
        )
    ]
    for copy in inputs:
        copy.start()
    for n in range(NCHUNK):
        tile_copy(n).start()

    placed[...] = jnp.zeros_like(placed)
    for copy in inputs:
        copy.wait()
    own = x_ref[...]
    slabs[j] = jnp.concatenate([own[:, :128], own[:, 128:]], axis=0)
    pl.semaphore_wait(barrier, 2 * (GROUP - 1) + jnp.where(far, GROUP, 0))

    def send(source, target, n, peer):
        return pltpu.make_async_remote_copy(
            src_ref=source,
            dst_ref=target,
            send_sem=send_sem.at[n],
            recv_sem=recv_sem.at[n],
            device_id={"grid": peer},
            device_id_type=MESH,
        )

    def sum_block(side, k):
        return acc.at[side, pl.ds(pl.multiple_of(k * 8, 8), 8)]

    first = [1, 0, 3, 2, 5, 4, 7, 6]
    swapped = j + 1 - 2 * (j % 2)
    first_others = []
    for n in range(GROUP - 1):
        k = n + jnp.where(n >= swapped, 1, 0)
        first_others.append(k + 1 - 2 * (k % 2))

    x_rows = [send(slabs.at[j], slabs.at[j], 0, peer) for peer in row_peers]
    x_cols = [send(slabs.at[j], slabs.at[GROUP + j], 1, peer) for peer in owners]
    sum_rows = [
        send(sum_block(0, k), sums.at[j], 2, a * GROUP + k) for k in first_others
    ]
    sum_cols = [
        send(sum_block(1, k), sums.at[GROUP + j], 3, c * GROUP + k) for k in first
    ]

    def several(buffer, count, n):
        part = buffer.at[pl.ds(0, count)]
        return send(part, part, n, row_peers[0])

    for copy in x_cols + x_rows:
        copy.start()

    def place(side, first):
        for k in range(GROUP):
            slab = slabs[first + k].astype(jnp.float32)
            block = jnp.concatenate([slab[:8], slab[8:]], axis=1)
            blank = jnp.zeros_like(block)
            low = jnp.concatenate([block, blank], axis=0).astype(jnp.bfloat16)
            high = jnp.concatenate([blank, block], axis=0).astype(jnp.bfloat16)
            for t in range(GROUP):
                rows = pl.ds(t // 2 * 16, 16)
                placed[side, GROUP * k + t, rows, :] = high if t % 2 else low

    live_count = count_ref[0]

    def coords(slot):
        return rows_ref[slot] - a * GROUP, cols_ref[slot] - c * GROUP

    def spread(side, slot, source, target):
        return placed[side, jnp.where(slot < live_count, GROUP * source + target, DEAD)]

    several(slabs, GROUP - 1, 0).wait_recv()
    place(0, 0)

    def mirror(n, total):
        for t in range(8):
            if t % CHUNK == 0:
                tile_copy(n * 1 + t // CHUNK).wait()
            slot = n * 8 + t
            r, q = coords(slot)
            total += jnp.dot(
                spread(0, slot, r, q), tiles[slot], preferred_element_type=jnp.float32
            )
        return total

    acc[1] = lax.fori_loop(0, 6, mirror, jnp.zeros((ROWS, B), jnp.float32))

    @pl.when(far)
    def _():
        for copy in sum_cols:
            copy.start()
        several(slabs, GROUP, 1).wait_recv()

    place(1, jnp.where(far, GROUP, 0))

    total = jnp.where(far, 0.0, acc[1])

    def direct(n, total):
        for t in range(8):
            slot = n * 8 + t
            r, q = coords(slot)
            total += lax.dot_general(
                spread(1, slot, q, r),
                tiles[slot],
                (((1,), (1,)), ((), ())),
                preferred_element_type=jnp.float32,
            )
        return total

    acc[0] = lax.fori_loop(0, 6, direct, total)

    for copy in sum_rows:
        copy.start()
    sums[j] = acc[0, pl.ds(pl.multiple_of(j * 8, 8), 8), :]
    several(sums, GROUP - 1, 3).wait_recv()
    result = sums[GROUP + 1]
    for k in range(GROUP + 2, 2 * GROUP):
        result += sums[k]
    several(sums, GROUP - 1, 2).wait_recv()
    for k in range(GROUP):
        result += sums[k]
    out_ref[...] = result

    several(slabs, GROUP - 1, 0).wait_send()
    several(slabs, GROUP - 1, 1).wait_send()
    several(sums, GROUP - 1, 2).wait_send()

    @pl.when(far)
    def _():
        several(sums, GROUP, 3).wait_send()


def per_device(vectors, tile_blocks, tile_rows, tile_cols, tile_counts):
    hbm = pl.BlockSpec(memory_space=pltpu.HBM)
    staged = [
        pltpu.with_memory_space_constraint(array, pltpu.HBM)
        for array in (vectors, tile_blocks, tile_rows, tile_cols)
    ]
    return pl.pallas_call(
        kernel,
        out_shape=pltpu.VMEM((8, B), jnp.float32),
        in_specs=[hbm] * 4 + [pl.BlockSpec(memory_space=pltpu.SMEM)],
        out_specs=pl.BlockSpec(memory_space=pltpu.VMEM),
        scratch_shapes=[
            pltpu.VMEM((8, B), jnp.bfloat16),
            pltpu.SMEM((SLOTS,), jnp.int32),
            pltpu.SMEM((SLOTS,), jnp.int32),
            pltpu.VMEM((SLOTS, B, B), jnp.bfloat16),
            pltpu.VMEM((2 * GROUP, 16, 128), jnp.bfloat16),
            pltpu.VMEM((2, DEAD + 1, ROWS, B), jnp.bfloat16),
            pltpu.VMEM((2, ROWS, B), jnp.float32),
            pltpu.VMEM((2 * GROUP, 8, B), jnp.float32),
            pltpu.SemaphoreType.DMA((3,)),
            pltpu.SemaphoreType.DMA((NCHUNK,)),
            pltpu.SemaphoreType.DMA((4,)),
            pltpu.SemaphoreType.DMA((4,)),
        ],
        compiler_params=pltpu.CompilerParams(
            collective_id=0, has_side_effects=True, vmem_limit_bytes=32 * 1024 * 1024
        ),
        cost_estimate=pl.CostEstimate(
            flops=4 * SLOTS * B * B * 8, bytes_accessed=SLOTS * B * B * 2, transcendentals=0
        ),
    )(*staged, tile_counts)


def solution(mesh):
    return jax.shard_map(
        per_device,
        mesh=mesh,
        in_specs=(P("vec", "grid"), P("grid", None, None), P("grid"), P("grid"), P("grid")),
        out_specs=P("vec", "grid"),
        check_vma=False,
    )
```

```python
import jax
import jax.numpy as jnp
from jax import lax
from jax.experimental import pallas as pl
from jax.experimental.pallas import tpu as pltpu
from jax.sharding import PartitionSpec as P

B = 256
GROUP = 8
NRANGE = 16
STEP = NRANGE // GROUP
SLOTS = 48
CHUNK = 8
NCHUNK = SLOTS // CHUNK
ROWS = GROUP * 8
DEAD = GROUP * GROUP
MESH = pl.DeviceIdType.MESH


def kernel(
    x_hbm,
    tiles_ref,
    rows_hbm,
    cols_hbm,
    count_ref,
    out_ref,
    x_ref,
    rows_ref,
    cols_ref,
    tiles,
    slabs,
    placed,
    acc,
    sums,
    in_sem,
    tile_sem,
    send_sem,
    recv_sem,
):
    me = lax.axis_index("grid")
    a = me // GROUP
    j = me % GROUP
    c = (a + STEP * j) % NRANGE
    far = j != 0

    def tile_copy(n):
        part = pl.ds(n * CHUNK, CHUNK)
        return pltpu.make_async_copy(tiles_ref.at[part], tiles.at[part], tile_sem.at[n])

    spots = [
        (j // 2 + x) % (GROUP // 2) * 2 + (j + core) % 2
        for x in (2, 1, 3, 0)
        for core in (0, 1)
    ]
    near = [k for n, k in enumerate(spots) if n != GROUP - 2]
    row_peers = [a * GROUP + k for k in near]
    owners = [
        ((a + NRANGE - STEP * d) % NRANGE) * GROUP + d for d in (4, 3, 5, 2, 6, 1, 7)
    ]
    col_peers = [c * GROUP + k for k in spots]

    barrier = pltpu.get_barrier_semaphore()

    @pl.when(far)
    def _():
        for peer in col_peers:
            pl.semaphore_signal(
                barrier, inc=1, device_id={"grid": peer}, device_id_type=MESH
            )

    for peer in owners + row_peers:
        pl.semaphore_signal(barrier, inc=1, device_id={"grid": peer}, device_id_type=MESH)

    inputs = [
        pltpu.make_async_copy(source, target, in_sem.at[n])
        for n, (source, target) in enumerate(
            [(x_hbm, x_ref), (rows_hbm, rows_ref), (cols_hbm, cols_ref)]
        )
    ]
    for copy in inputs:
        copy.start()
    for n in range(NCHUNK):
        tile_copy(n).start()

    placed[...] = jnp.zeros_like(placed)
    for copy in inputs:
        copy.wait()
    own = x_ref[...]
    slabs[j] = jnp.concatenate([own[:, :128], own[:, 128:]], axis=0)
    pl.semaphore_wait(barrier, 2 * (GROUP - 1) + jnp.where(far, GROUP, 0))

    def send(source, target, n, peer):
        return pltpu.make_async_remote_copy(
            src_ref=source,
            dst_ref=target,
            send_sem=send_sem.at[n],
            recv_sem=recv_sem.at[n],
            device_id={"grid": peer},
            device_id_type=MESH,
        )

    def sum_block(side, k):
        return acc.at[side, pl.ds(pl.multiple_of(k * 8, 8), 8)]

    first = [1, 0, 3, 2, 5, 4, 7, 6]
    swapped = j + 1 - 2 * (j % 2)
    first_others = []
    for n in range(GROUP - 1):
        k = n + jnp.where(n >= swapped, 1, 0)
        first_others.append(k + 1 - 2 * (k % 2))

    x_rows = [send(slabs.at[j], slabs.at[j], 0, peer) for peer in row_peers]
    x_cols = [send(slabs.at[j], slabs.at[GROUP + j], 1, peer) for peer in owners]
    sum_rows = [
        send(sum_block(0, k), sums.at[j], 2, a * GROUP + k) for k in first_others
    ]
    sum_cols = [
        send(sum_block(1, k), sums.at[GROUP + j], 3, c * GROUP + k) for k in first
    ]

    def several(buffer, count, n):
        part = buffer.at[pl.ds(0, count)]
        return send(part, part, n, row_peers[0])

    for copy in x_cols + x_rows:
        copy.start()

    def place(side, first):
        for k in range(GROUP):
            slab = slabs[first + k].astype(jnp.float32)
            block = jnp.concatenate([slab[:8], slab[8:]], axis=1)
            blank = jnp.zeros_like(block)
            low = jnp.concatenate([block, blank], axis=0).astype(jnp.bfloat16)
            high = jnp.concatenate([blank, block], axis=0).astype(jnp.bfloat16)
            for t in range(GROUP):
                rows = pl.ds(t // 2 * 16, 16)
                placed[side, GROUP * k + t, rows, :] = high if t % 2 else low

    live_count = count_ref[0]

    def coords(slot):
        return rows_ref[slot] - a * GROUP, cols_ref[slot] - c * GROUP

    def spread(side, slot, source, target):
        return placed[side, jnp.where(slot < live_count, GROUP * source + target, DEAD)]

    several(slabs, GROUP - 1, 0).wait_recv()
    place(0, 0)

    def mirror(n, total):
        for t in range(8):
            if t % CHUNK == 0:
                tile_copy(n * 1 + t // CHUNK).wait()
            slot = n * 8 + t
            r, q = coords(slot)
            total += jnp.dot(
                spread(0, slot, r, q), tiles[slot], preferred_element_type=jnp.float32
            )
        return total

    acc[1] = lax.fori_loop(0, 6, mirror, jnp.zeros((ROWS, B), jnp.float32))

    @pl.when(far)
    def _():
        for copy in sum_cols:
            copy.start()
        several(slabs, GROUP, 1).wait_recv()

    place(1, jnp.where(far, GROUP, 0))

    total = jnp.where(far, 0.0, acc[1])

    def direct(n, total):
        for t in range(8):
            slot = n * 8 + t
            r, q = coords(slot)
            total += lax.dot_general(
                spread(1, slot, q, r),
                tiles[slot],
                (((1,), (1,)), ((), ())),
                preferred_element_type=jnp.float32,
            )
        return total

    acc[0] = lax.fori_loop(0, 6, direct, total)

    for copy in sum_rows:
        copy.start()
    sums[j] = acc[0, pl.ds(pl.multiple_of(j * 8, 8), 8), :]

    several(slabs, GROUP - 1, 0).wait_send()
    several(slabs, GROUP - 1, 1).wait_send()

    @pl.when(far)
    def _():
        several(sums, GROUP, 3).wait_send()

    several(sums, GROUP - 1, 2).wait_send()
    several(sums, GROUP - 1, 3).wait_recv()
    result = sums[GROUP + 1]
    for k in range(GROUP + 2, 2 * GROUP):
        result += sums[k]
    several(sums, GROUP - 1, 2).wait_recv()
    for k in range(GROUP):
        result += sums[k]
    out_ref[...] = result


def per_device(vectors, tile_blocks, tile_rows, tile_cols, tile_counts):
    hbm = pl.BlockSpec(memory_space=pltpu.HBM)
    staged = [
        pltpu.with_memory_space_constraint(array, pltpu.HBM)
        for array in (vectors, tile_blocks, tile_rows, tile_cols)
    ]
    return pl.pallas_call(
        kernel,
        out_shape=pltpu.VMEM((8, B), jnp.float32),
        in_specs=[hbm] * 4 + [pl.BlockSpec(memory_space=pltpu.SMEM)],
        out_specs=pl.BlockSpec(memory_space=pltpu.VMEM),
        scratch_shapes=[
            pltpu.VMEM((8, B), jnp.bfloat16),
            pltpu.SMEM((SLOTS,), jnp.int32),
            pltpu.SMEM((SLOTS,), jnp.int32),
            pltpu.VMEM((SLOTS, B, B), jnp.bfloat16),
            pltpu.VMEM((2 * GROUP, 16, 128), jnp.bfloat16),
            pltpu.VMEM((2, DEAD + 1, ROWS, B), jnp.bfloat16),
            pltpu.VMEM((2, ROWS, B), jnp.float32),
            pltpu.VMEM((2 * GROUP, 8, B), jnp.float32),
            pltpu.SemaphoreType.DMA((3,)),
            pltpu.SemaphoreType.DMA((NCHUNK,)),
            pltpu.SemaphoreType.DMA((4,)),
            pltpu.SemaphoreType.DMA((4,)),
        ],
        compiler_params=pltpu.CompilerParams(
            collective_id=0, has_side_effects=True, vmem_limit_bytes=32 * 1024 * 1024
        ),
        cost_estimate=pl.CostEstimate(
            flops=4 * SLOTS * B * B * 8, bytes_accessed=SLOTS * B * B * 2, transcendentals=0
        ),
    )(*staged, tile_counts)


def solution(mesh):
    return jax.shard_map(
        per_device,
        mesh=mesh,
        in_specs=(P("vec", "grid"), P("grid", None, None), P("grid"), P("grid"), P("grid")),
        out_specs=P("vec", "grid"),
        check_vma=False,
    )
```

```python
import jax
import jax.numpy as jnp
from jax import lax
from jax.experimental import pallas as pl
from jax.experimental.pallas import tpu as pltpu
from jax.sharding import PartitionSpec as P

B = 256
GROUP = 8
NRANGE = 16
STEP = NRANGE // GROUP
SLOTS = 48
CHUNK = 8
NCHUNK = SLOTS // CHUNK
ROWS = GROUP * 8
DEAD = GROUP * GROUP
MESH = pl.DeviceIdType.MESH


def kernel(
    x_hbm,
    tiles_ref,
    rows_hbm,
    cols_hbm,
    count_ref,
    out_ref,
    x_ref,
    rows_ref,
    cols_ref,
    tiles,
    slabs,
    placed,
    acc,
    sums,
    in_sem,
    tile_sem,
    send_sem,
    recv_sem,
):
    me = lax.axis_index("grid")
    a = me // GROUP
    j = me % GROUP
    c = (a + STEP * j) % NRANGE
    far = j != 0

    def tile_copy(n):
        part = pl.ds(n * CHUNK, CHUNK)
        return pltpu.make_async_copy(tiles_ref.at[part], tiles.at[part], tile_sem.at[n])

    spots = [
        (j // 2 + x) % (GROUP // 2) * 2 + (j + core) % 2
        for x in (2, 1, 3, 0)
        for core in (0, 1)
    ]
    near = [k for n, k in enumerate(spots) if n != GROUP - 2]
    row_peers = [a * GROUP + k for k in near]
    owners = [
        ((a + NRANGE - STEP * d) % NRANGE) * GROUP + d for d in (4, 3, 5, 2, 6, 1, 7)
    ]
    col_peers = [c * GROUP + k for k in spots]

    barrier = pltpu.get_barrier_semaphore()

    @pl.when(far)
    def _():
        for peer in col_peers:
            pl.semaphore_signal(
                barrier, inc=1, device_id={"grid": peer}, device_id_type=MESH
            )

    for peer in owners + row_peers:
        pl.semaphore_signal(barrier, inc=1, device_id={"grid": peer}, device_id_type=MESH)

    inputs = [
        pltpu.make_async_copy(source, target, in_sem.at[n])
        for n, (source, target) in enumerate(
            [(x_hbm, x_ref), (rows_hbm, rows_ref), (cols_hbm, cols_ref)]
        )
    ]
    for copy in inputs:
        copy.start()
    for n in range(NCHUNK):
        tile_copy(n).start()

    placed[...] = jnp.zeros_like(placed)
    for copy in inputs:
        copy.wait()
    own = x_ref[...]
    slabs[j] = jnp.concatenate([own[:, :128], own[:, 128:]], axis=0)
    pl.semaphore_wait(barrier, 2 * (GROUP - 1) + jnp.where(far, GROUP, 0))

    def send(source, target, n, peer):
        return pltpu.make_async_remote_copy(
            src_ref=source,
            dst_ref=target,
            send_sem=send_sem.at[n],
            recv_sem=recv_sem.at[n],
            device_id={"grid": peer},
            device_id_type=MESH,
        )

    def sum_block(side, k):
        return acc.at[side, pl.ds(pl.multiple_of(k * 8, 8), 8)]

    first = [1, 0, 3, 2, 5, 4, 7, 6]
    swapped = j + 1 - 2 * (j % 2)
    first_others = []
    for n in range(GROUP - 1):
        k = n + jnp.where(n >= swapped, 1, 0)
        first_others.append(k + 1 - 2 * (k % 2))

    x_rows = [send(slabs.at[j], slabs.at[j], 0, peer) for peer in row_peers]
    x_cols = [send(slabs.at[j], slabs.at[GROUP + j], 1, peer) for peer in owners]
    sum_rows = [
        send(sum_block(0, k), sums.at[j], 2, a * GROUP + k) for k in first_others
    ]
    sum_cols = [
        send(sum_block(1, k), sums.at[GROUP + j], 3, c * GROUP + k) for k in first
    ]

    def several(buffer, count, n):
        part = buffer.at[pl.ds(0, count)]
        return send(part, part, n, row_peers[0])

    for copy in x_rows + x_cols:
        copy.start()

    def place(side, first):
        for k in range(GROUP):
            slab = slabs[first + k].astype(jnp.float32)
            block = jnp.concatenate([slab[:8], slab[8:]], axis=1)
            blank = jnp.zeros_like(block)
            low = jnp.concatenate([block, blank], axis=0).astype(jnp.bfloat16)
            high = jnp.concatenate([blank, block], axis=0).astype(jnp.bfloat16)
            for t in range(GROUP):
                rows = pl.ds(t // 2 * 16, 16)
                placed[side, GROUP * k + t, rows, :] = high if t % 2 else low

    live_count = count_ref[0]

    def coords(slot):
        return rows_ref[slot] - a * GROUP, cols_ref[slot] - c * GROUP

    def spread(side, slot, source, target):
        return placed[side, jnp.where(slot < live_count, GROUP * source + target, DEAD)]

    several(slabs, GROUP - 1, 0).wait_recv()
    place(0, 0)

    def mirror(n, total):
        for t in range(8):
            if t % CHUNK == 0:
                tile_copy(n * 1 + t // CHUNK).wait()
            slot = n * 8 + t
            r, q = coords(slot)
            total += jnp.dot(
                spread(0, slot, r, q), tiles[slot], preferred_element_type=jnp.float32
            )
        return total

    acc[1] = lax.fori_loop(0, 6, mirror, jnp.zeros((ROWS, B), jnp.float32))

    @pl.when(far)
    def _():
        for copy in sum_cols:
            copy.start()
        several(slabs, GROUP, 1).wait_recv()

    place(1, jnp.where(far, GROUP, 0))

    total = jnp.where(far, 0.0, acc[1])

    def direct(n, total):
        for t in range(8):
            slot = n * 8 + t
            r, q = coords(slot)
            total += lax.dot_general(
                spread(1, slot, q, r),
                tiles[slot],
                (((1,), (1,)), ((), ())),
                preferred_element_type=jnp.float32,
            )
        return total

    acc[0] = lax.fori_loop(0, 6, direct, total)

    for copy in sum_rows:
        copy.start()
    sums[j] = acc[0, pl.ds(pl.multiple_of(j * 8, 8), 8), :]
    several(sums, GROUP - 1, 3).wait_recv()
    result = sums[GROUP + 1]
    for k in range(GROUP + 2, 2 * GROUP):
        result += sums[k]
    several(sums, GROUP - 1, 2).wait_recv()
    for k in range(GROUP):
        result += sums[k]
    out_ref[...] = result

    several(slabs, GROUP - 1, 0).wait_send()
    several(slabs, GROUP - 1, 1).wait_send()
    several(sums, GROUP - 1, 2).wait_send()

    @pl.when(far)
    def _():
        several(sums, GROUP, 3).wait_send()


def per_device(vectors, tile_blocks, tile_rows, tile_cols, tile_counts):
    hbm = pl.BlockSpec(memory_space=pltpu.HBM)
    staged = [
        pltpu.with_memory_space_constraint(array, pltpu.HBM)
        for array in (vectors, tile_blocks, tile_rows, tile_cols)
    ]
    return pl.pallas_call(
        kernel,
        out_shape=pltpu.VMEM((8, B), jnp.float32),
        in_specs=[hbm] * 4 + [pl.BlockSpec(memory_space=pltpu.SMEM)],
        out_specs=pl.BlockSpec(memory_space=pltpu.VMEM),
        scratch_shapes=[
            pltpu.VMEM((8, B), jnp.bfloat16),
            pltpu.SMEM((SLOTS,), jnp.int32),
            pltpu.SMEM((SLOTS,), jnp.int32),
            pltpu.VMEM((SLOTS, B, B), jnp.bfloat16),
            pltpu.VMEM((2 * GROUP, 16, 128), jnp.bfloat16),
            pltpu.VMEM((2, DEAD + 1, ROWS, B), jnp.bfloat16),
            pltpu.VMEM((2, ROWS, B), jnp.float32),
            pltpu.VMEM((2 * GROUP, 8, B), jnp.float32),
            pltpu.SemaphoreType.DMA((3,)),
            pltpu.SemaphoreType.DMA((NCHUNK,)),
            pltpu.SemaphoreType.DMA((4,)),
            pltpu.SemaphoreType.DMA((4,)),
        ],
        compiler_params=pltpu.CompilerParams(
            collective_id=0, has_side_effects=True, vmem_limit_bytes=32 * 1024 * 1024
        ),
        cost_estimate=pl.CostEstimate(
            flops=4 * SLOTS * B * B * 8, bytes_accessed=SLOTS * B * B * 2, transcendentals=0
        ),
    )(*staged, tile_counts)


def solution(mesh):
    return jax.shard_map(
        per_device,
        mesh=mesh,
        in_specs=(P("vec", "grid"), P("grid", None, None), P("grid"), P("grid"), P("grid")),
        out_specs=P("vec", "grid"),
        check_vma=False,
    )
```
